768 devices in a mesh: dp: 12 (over z_lo, x), seq: 32 (over y, z_hi), grp: 2 (over core).
Axes of the slice: x: 4, y: 8, z: 12 (z_hi: 4, z_lo: 3; z = z_hi * 3 + z_lo), core: 2. Of those that a mesh axis runs over, the one named last changes fastest.
Arguments:
- text_proj: bfloat16 [3, 384, 12, 128, 128], P(None, 'dp', None, ('seq', 'grp')), may hold values from -50 to 50
- image_proj: bfloat16 [3, 384, 12, 160, 128], P(None, ('dp', 'seq'), None, 'grp'), may hold values from -50 to 50
- text_grad: bfloat16 [384, 12, 128, 128], P('dp', None, ('seq', 'grp')), may hold values from -15 to 15
- image_grad: bfloat16 [384, 12, 160, 128], P(('dp', 'seq'), None, 'grp'), may hold values from -15 to 15
- text_lengths: int32 [384], P(('dp', 'seq')), may hold values from 1 to 128
- norm_gains: float32 [2, 2, 128], replicated, may hold values from 0.7 to 5.2
Outputs:
- text_out: bfloat16 [384, 12, 128, 128], P('dp', None, ('seq', 'grp'))
- image_out: bfloat16 [384, 12, 160, 128], P(('dp', 'seq'), None, 'grp')
- text_proj_grad: bfloat16 [3, 384, 12, 128, 128], P(None, 'dp', None, ('seq', 'grp'))
- image_proj_grad: bfloat16 [3, 384, 12, 160, 128], P(None, ('dp', 'seq'), None, 'grp')
- gain_grad: float32 [2, 2, 128], replicated
The draws below stay inside these ranges and needn't reach their ends.
All inputs are finite; a program needn't handle non-finite values.
Results may differ from the reference program's by a relative error of at most 0.025.
The reference program's roundings to bfloat16 on the way (of `normed`, `rounded_probs`, `grad_value`, `grad_scores` and `grad_normed`) count: a program that leaves them out, or rounds other values in their place, can miss the bound.
Values may be sent and summed in bfloat16 or wider, within the bound.
A program may use at most 32 MiB of HBM per device.

```python
import math
import jax
import jax.numpy as jnp
from jax import lax

HEADS = 12
HD = 128
TXT = 128
IMG = 160
SAMPLES = 384
JOINT = 288


def scaled_noise(key, shape):
    noise_key, scale_key = jax.random.split(key)
    values = jax.random.truncated_normal(noise_key, -5.0, 5.0, shape, jnp.float32)
    row_scale = jnp.exp(jax.random.uniform(scale_key, shape[:-1] + (1,), jnp.float32, 0.0, math.log(10.0)))
    component = jnp.arange(3).reshape(3, 1, 1, 1, 1)
    return values * jnp.where(component < 2, row_scale, 1.0)


def draw_text_proj(key, part):
    values = scaled_noise(jax.random.fold_in(key, 11), (3, SAMPLES, HEADS, TXT, HD))
    return values.astype(jnp.bfloat16)


def draw_image_proj(key, part):
    noise_key = jax.random.fold_in(jax.random.fold_in(key, 13), 0)
    values = scaled_noise(noise_key, (3, SAMPLES, HEADS, IMG, HD))
    return values.astype(jnp.bfloat16)


def ramped(key, shape, offset):
    values = jax.random.truncated_normal(key, -4.0, 4.0, shape, jnp.float32)
    along_samples = 1.0 + 2.0 * jnp.arange(SAMPLES, dtype=jnp.float32) / max(SAMPLES - 1, 1)
    along_positions = 1.0 + 2.0 * (offset + jnp.arange(shape[2], dtype=jnp.float32)) / (JOINT - 1)
    return values * 0.4 * along_samples[:, None, None, None] * along_positions[None, None, :, None]


def draw_text_grad(key, part):
    return ramped(jax.random.fold_in(key, 23), (SAMPLES, HEADS, TXT, HD), 0).astype(jnp.bfloat16)


def draw_image_grad(key, part):
    return ramped(jax.random.fold_in(key, 29), (SAMPLES, HEADS, IMG, HD), TXT).astype(jnp.bfloat16)


def draw_norm_gains(key, part):
    gain_key = jax.random.fold_in(key, 37)
    return jnp.exp(jax.random.uniform(gain_key, (2, 2, HD), jnp.float32, math.log(0.7), math.log(1.5)))


def with_ends(entries, rng, low, top_value):
    dims = entries.shape
    index_at = [jax.random.randint(jax.random.fold_in(rng, axis), (), 0, dims[axis]) for axis in range(len(dims))]
    entries = entries.at[tuple(index_at)].set(low)
    longest = dims.index(max(dims))
    index_at[longest] = (index_at[longest] + 1) % dims[longest]
    return entries.at[tuple(index_at)].set(top_value)


def setup_inputs(seed: int = 0) -> dict:
    seeds = jax.random.split(jax.random.key(seed), 7)
    text_proj = draw_text_proj(jax.random.fold_in(seeds[6], 71), 0)
    image_proj = draw_image_proj(jax.random.fold_in(seeds[6], 71), 0)
    text_grad = draw_text_grad(jax.random.fold_in(seeds[6], 71), 0)
    image_grad = draw_image_grad(jax.random.fold_in(seeds[6], 71), 0)
    text_lengths = with_ends(jax.random.randint(seeds[4], (SAMPLES,), 1, TXT + 1), jax.random.fold_in(seeds[4], 1), 1, TXT).astype(jnp.int32)
    norm_gains = draw_norm_gains(jax.random.fold_in(seeds[6], 71), 0)
    return dict(text_proj=text_proj, image_proj=image_proj, text_grad=text_grad, image_grad=image_grad, text_lengths=text_lengths, norm_gains=norm_gains)


EPSILON = 1e-06
MASKED = -1e+30

def normalize(raw_vals, is_text, norm_gains):
    inverse = lax.rsqrt(lax.optimization_barrier(jnp.mean(raw_vals * raw_vals, axis=-1, keepdims=True)) + EPSILON)
    unit_vec = raw_vals * inverse
    gain_map = jnp.where(is_text[None, :, None], norm_gains[0][:, None, :], norm_gains[1][:, None, :])
    return (unit_vec, inverse, gain_map)

def forward(queries, key_rows, value_rows, key_valid):
    factor = queries.shape[-1] ** (-0.5)
    scores = jnp.einsum('nqd,nkd->nqk', queries.astype(jnp.float32), key_rows.astype(jnp.float32)) * factor
    scores = jnp.where(key_valid[:, None, :], scores, MASKED)
    row_max = lax.optimization_barrier(jnp.max(scores, axis=-1, keepdims=True))
    exponent = jnp.exp(scores - row_max)
    attn_probs = exponent / lax.optimization_barrier(jnp.sum(exponent, axis=-1, keepdims=True))
    rounded_probs = attn_probs.astype(jnp.bfloat16)
    attn_local = jnp.einsum('nqk,nkd->nqd', rounded_probs.astype(jnp.float32), value_rows.astype(jnp.float32))
    return (attn_probs, rounded_probs, attn_local)

def backward(queries, key_rows, value_rows, attn_probs, rounded_probs, grad_out):
    factor = queries.shape[-1] ** (-0.5)
    grad_value = jnp.einsum('nqk,nqd->nkd', rounded_probs.astype(jnp.float32), grad_out.astype(jnp.float32)).astype(jnp.bfloat16)
    grad_probs = jnp.einsum('nqd,nkd->nqk', grad_out.astype(jnp.float32), value_rows.astype(jnp.float32))
    row_delta = lax.optimization_barrier(jnp.sum(attn_probs * grad_probs, axis=-1, keepdims=True))
    grad_scores = (attn_probs * (grad_probs - row_delta) * factor).astype(jnp.bfloat16)
    grad_query = jnp.einsum('nqk,nkd->nqd', grad_scores.astype(jnp.float32), key_rows.astype(jnp.float32)).astype(jnp.bfloat16)
    grad_key = jnp.einsum('nqk,nqd->nkd', grad_scores.astype(jnp.float32), queries.astype(jnp.float32)).astype(jnp.bfloat16)
    return (grad_query, grad_key, grad_value)

def reference(text_proj, image_proj, text_grad, image_grad, text_lengths, norm_gains):
    joint_len = TXT + IMG
    position = jnp.arange(joint_len, dtype=jnp.int32)
    is_text = position < TXT
    text_flag = is_text.astype(jnp.float32)

    def per_sample(sample_item):
        text_block, image_block, text_cot, image_cot, text_length = sample_item
        sample_block = jnp.concatenate([text_block, image_block], axis=2)
        cotangent = jnp.concatenate([text_cot, image_cot], axis=1)
        raw_vals = sample_block[:2].astype(jnp.float32)
        unit_vec, inverse, gain_map = normalize(raw_vals, is_text, norm_gains)
        normed = (unit_vec * gain_map[:, None]).astype(jnp.bfloat16)
        key_valid = (position >= TXT) | (position < text_length)
        key_valid = jnp.broadcast_to(key_valid[None, :], (sample_block.shape[1], joint_len))
        attn_probs, rounded_probs, attn_local = forward(normed[0], normed[1], sample_block[2], key_valid)
        grad_query, grad_key, grad_value = backward(normed[0], normed[1], sample_block[2], attn_probs, rounded_probs, cotangent)
        grad_normed = jnp.stack([grad_query, grad_key]).astype(jnp.float32)
        per_position = lax.optimization_barrier(jnp.sum(grad_normed * unit_vec, axis=1))
        gain_part = jnp.stack([jnp.einsum('l,qld->qd', text_flag, per_position), jnp.einsum('l,qld->qd', 1.0 - text_flag, per_position)])
        grad_unit = grad_normed * gain_map[:, None]
        grad_raw = inverse * (grad_unit - unit_vec * lax.optimization_barrier(jnp.mean(grad_unit * unit_vec, axis=-1, keepdims=True)))
        gradients = jnp.concatenate([grad_raw.astype(jnp.bfloat16), grad_value[None]], axis=0)
        attn_rounded = attn_local.astype(jnp.bfloat16)
        return (attn_rounded[:, :TXT], attn_rounded[:, TXT:], gradients[:, :, :TXT], gradients[:, :, TXT:], gain_part)
    text_out, image_out, text_grads, image_grads, gain_parts = lax.map(per_sample, (jnp.moveaxis(text_proj, 1, 0), jnp.moveaxis(image_proj, 1, 0), text_grad, image_grad, text_lengths))
    gain_grad = lax.optimization_barrier(jnp.sum(gain_parts, axis=0)) / text_proj.shape[1]
    return (text_out, image_out, jnp.moveaxis(text_grads, 0, 1), jnp.moveaxis(image_grads, 0, 1), gain_grad)
```

```python
import functools

import jax
import jax.numpy as jnp
from jax import lax
from jax.experimental import pallas as pl
from jax.experimental.pallas import tpu as pltpu
from jax.sharding import PartitionSpec as P

EPSILON = 1e-06
MASKED = -1e30
MESH_ID = pl.DeviceIdType.MESH
NZ = 4
HEADS_PER_STEP = 2


def dot(a, b, contract_a, contract_b):
    return lax.dot_general(
        a, b, (((contract_a,), (contract_b,)), ((), ())), preferred_element_type=jnp.float32
    )


def unit_parts(raw):
    raw_vals = raw.astype(jnp.float32)
    inverse = lax.rsqrt(jnp.mean(raw_vals * raw_vals, axis=-1, keepdims=True) + EPSILON)
    return raw_vals * inverse, inverse


def attend_head(query_raw, key_raw, value, cotangent, bias, gains, text_rows):
    total, size = query_raw.shape
    factor = size**-0.5

    def gain_rows(c):
        return jnp.concatenate(
            [
                jnp.broadcast_to(gains[0, c][None, :], (text_rows, size)),
                jnp.broadcast_to(gains[1, c][None, :], (total - text_rows, size)),
            ],
            axis=0,
        )

    query_unit, query_inverse = unit_parts(query_raw)
    key_unit, key_inverse = unit_parts(key_raw)
    query_gain, key_gain = gain_rows(0), gain_rows(1)
    query = (query_unit * query_gain).astype(jnp.bfloat16)
    key = (key_unit * key_gain).astype(jnp.bfloat16)

    scores = jnp.where(bias < 0, MASKED, dot(query, key, 1, 1) * factor)
    exponent = jnp.exp(scores - jnp.max(scores, axis=-1, keepdims=True))
    probs = exponent * (1.0 / jnp.sum(exponent, axis=-1, keepdims=True))
    rounded = probs.astype(jnp.bfloat16)
    attention = dot(rounded, value, 1, 0).astype(jnp.bfloat16)
    grad_value = dot(rounded, cotangent, 0, 0).astype(jnp.bfloat16)
    grad_probs = dot(cotangent, value, 1, 1)
    row_delta = jnp.sum(probs * grad_probs, axis=-1, keepdims=True)
    grad_scores = (probs * (grad_probs - row_delta) * factor).astype(jnp.bfloat16)

    def raw_gradient(grad_normed, unit, inverse, gain):
        grad_normed = grad_normed.astype(jnp.bfloat16).astype(jnp.float32)
        term = grad_normed * unit
        text_part = jnp.sum(term[:text_rows], axis=0, keepdims=True)
        image_part = jnp.sum(term[text_rows:], axis=0, keepdims=True)
        mean = jnp.mean(term * gain, axis=-1, keepdims=True)
        grad_raw = inverse * (grad_normed * gain - unit * mean)
        return grad_raw.astype(jnp.bfloat16), text_part, image_part

    grad_query, query_text, query_image = raw_gradient(
        dot(grad_scores, key, 1, 0), query_unit, query_inverse, query_gain
    )
    grad_key, key_text, key_image = raw_gradient(
        dot(grad_scores, query, 0, 0), key_unit, key_inverse, key_gain
    )
    parts = jnp.concatenate([query_text, key_text, query_image, key_image], axis=0)
    return (attention, grad_query, grad_key, grad_value), parts


def kernel(
    sizes,
    text_proj,
    text_grad,
    image_proj,
    image_grad,
    length,
    gains,
    text_out,
    text_proj_grad,
    image_out,
    image_proj_grad,
    gain_out,
    text_in,
    image_in,
    text_res,
    image_res,
    gain_part,
    gain_first,
    gain_mid,
    gain_second,
    text_send,
    text_recv,
    image_send,
    image_recv,
    back_send,
    back_recv,
    image_back_send,
    image_back_recv,
    gain_send,
    gain_recv,
):
    dp_count, seq_count, samples = sizes
    rows_y = seq_count // NZ
    dp, seq, grp = lax.axis_index("dp"), lax.axis_index("seq"), lax.axis_index("grp")
    other = 1 - grp
    owner_count = seq_count * 2
    me = seq * 2 + grp
    heads = text_in.shape[1]
    text_rows = owner_count * text_in.shape[3]
    image_rows = image_proj.shape[3]
    hps = HEADS_PER_STEP
    steps = heads // hps

    def seq_peer(k):
        y = lax.rem(seq // NZ + k // NZ, rows_y)
        z = lax.rem(lax.rem(seq, NZ) + lax.rem(k, NZ), NZ)
        return y * NZ + z

    def peer(k):
        return seq_peer(lax.rem(k, seq_count)), lax.rem(grp + k // seq_count, 2)

    def first_peer(k):
        return lax.rem(dp + k // 2, dp_count), lax.rem(grp + k, 2)

    def loop(low, high, body):
        def step(k, carry):
            body(k)
            return carry

        lax.fori_loop(low, high, step, 0)

    barrier = pltpu.get_barrier_semaphore()

    def greet(k):
        peer_seq, peer_grp = peer(k)
        pl.semaphore_signal(
            barrier, inc=1, device_id=(dp, peer_seq, peer_grp), device_id_type=MESH_ID
        )

    def greet_first(k):
        peer_dp, peer_grp = first_peer(k)
        pl.semaphore_signal(
            barrier, inc=1, device_id=(peer_dp, seq, peer_grp), device_id_type=MESH_ID
        )

    loop(1, owner_count, greet)
    loop(2, 2 * dp_count, greet_first)

    gain_part[...] = jnp.zeros_like(gain_part)
    pl.semaphore_wait(barrier, owner_count - 1 + 2 * dp_count - 2)

    def remote(src, dst, send, recv, target):
        return pltpu.make_async_remote_copy(
            src_ref=src,
            dst_ref=dst,
            send_sem=send,
            recv_sem=recv,
            device_id=target,
            device_id_type=MESH_ID,
        )

    all_heads = pl.ds(0, heads)
    given = pl.ds(pl.multiple_of(other * heads, heads), heads)
    kept = pl.ds(pl.multiple_of(grp * heads, heads), heads)
    my_rows = pl.ds(pl.multiple_of(grp * image_rows, image_rows), image_rows)
    other_rows = pl.ds(pl.multiple_of(other * image_rows, image_rows), image_rows)
    partner = (dp, seq, other)
    remote(
        image_proj.at[:, 0, given],
        image_in.at[pl.ds(0, 3), all_heads, my_rows],
        image_send.at[0],
        image_recv.at[0],
        partner,
    ).start()
    remote(
        image_grad.at[0, given],
        image_in.at[3, all_heads, my_rows],
        image_send.at[1],
        image_recv.at[1],
        partner,
    ).start()
    local_images = (
        pltpu.make_async_copy(
            image_proj.at[:, 0, kept],
            image_in.at[pl.ds(0, 3), all_heads, my_rows],
            image_recv.at[2],
        ),
        pltpu.make_async_copy(
            image_grad.at[0, kept], image_in.at[3, all_heads, my_rows], image_recv.at[3]
        ),
    )
    for copy in local_images:
        copy.start()

    def text_step(step):
        own = pl.ds(step * hps, hps)

        def ends(peer_seq, peer_grp):
            theirs = pl.ds(peer_grp * heads + step * hps, hps)
            return (
                (text_proj.at[:, peer_seq, theirs], text_in.at[pl.ds(0, 3), own, me]),
                (text_grad.at[peer_seq, theirs], text_in.at[3, own, me]),
            )

        for i, (src, dst) in enumerate(ends(seq, grp)):
            pltpu.make_async_copy(src, dst, text_recv.at[i, step]).start()

        def send(k):
            peer_seq, peer_grp = peer(k)
            for i, (src, dst) in enumerate(ends(peer_seq, peer_grp)):
                remote(
                    src,
                    dst,
                    text_send.at[i, step],
                    text_recv.at[i, step],
                    (dp, peer_seq, peer_grp),
                ).start()

        loop(1, owner_count, send)

    loop(0, steps, text_step)

    for copy in local_images:
        copy.wait()
    for i, part in enumerate((image_in.at[pl.ds(0, 3), all_heads, other_rows], image_in.at[3, all_heads, other_rows])):
        pltpu.make_async_copy(part, part, image_recv.at[i]).wait()

    total = text_rows + 2 * image_rows
    place = lax.broadcasted_iota(jnp.int32, (1, total), 1)
    bias = jnp.where((place >= text_rows) | (place < length[0]), 0.0, -1.0)

    def work(step):
        own = pl.ds(step * hps, hps)
        for i, part in enumerate((text_in.at[pl.ds(0, 3), own], text_in.at[3, own])):
            pltpu.make_async_copy(part, part, text_recv.at[i, step]).wait()
        for j in range(hps):
            head = step * hps + j
            rows = [
                jnp.concatenate(
                    [
                        text_in[c, head].reshape(text_rows, text_in.shape[-1]),
                        image_in[c, head],
                    ],
                    axis=0,
                )
                for c in range(4)
            ]
            results, parts = attend_head(*rows, bias, gains, text_rows)
            gain_part[...] += parts
            for c, result in enumerate(results):
                text_res[c, head] = result[:text_rows].reshape(text_res.shape[2:])
                image_res[c, head] = result[text_rows:]

        def back_ends(owner):
            there = pl.ds(grp * heads + step * hps, hps)
            return (
                (text_res.at[0, own, owner], text_out.at[seq, there]),
                (text_res.at[pl.ds(1, 3), own, owner], text_proj_grad.at[:, seq, there]),
            )

        def send_back(k):
            peer_seq, peer_grp = peer(k)
            for i, (src, dst) in enumerate(back_ends(peer_seq * 2 + peer_grp)):
                remote(
                    src, dst, back_send.at[i], back_recv.at[i], (dp, peer_seq, peer_grp)
                ).start()

        loop(1, owner_count, send_back)
        for i, (src, dst) in enumerate(back_ends(me)):
            pltpu.make_async_copy(src, dst, back_recv.at[i]).start()

    loop(0, steps, work)

    remote(
        image_res.at[0, all_heads, other_rows],
        image_out.at[0, kept],
        image_back_send.at[0],
        image_back_recv.at[0],
        partner,
    ).start()
    remote(
        image_res.at[pl.ds(1, 3), all_heads, other_rows],
        image_proj_grad.at[:, 0, kept],
        image_back_send.at[1],
        image_back_recv.at[1],
        partner,
    ).start()
    local_results = (
        pltpu.make_async_copy(
            image_res.at[0, all_heads, my_rows], image_out.at[0, kept], image_back_recv.at[2]
        ),
        pltpu.make_async_copy(
            image_res.at[pl.ds(1, 3), all_heads, my_rows],
            image_proj_grad.at[:, 0, kept],
            image_back_recv.at[3],
        ),
    )
    for copy in local_results:
        copy.start()

    first_me = dp * 2 + grp
    gain_first[first_me] = gain_part[...]

    def send_first(k):
        peer_dp, peer_grp = first_peer(k)
        remote(
            gain_part,
            gain_first.at[first_me],
            gain_send.at[0],
            gain_recv.at[0],
            (peer_dp, seq, peer_grp),
        ).start()

    loop(1, 2 * dp_count, send_first)
    first_others = gain_first.at[pl.ds(0, 2 * dp_count - 1)]
    pltpu.make_async_copy(first_others, first_others, gain_recv.at[0]).wait()
    mid = jnp.sum(gain_first[...], axis=0)
    gain_mid[...] = mid
    gain_second[seq] = mid

    def send_second(k):
        remote(
            gain_mid,
            gain_second.at[seq],
            gain_send.at[1],
            gain_recv.at[1],
            (dp, seq_peer(k), grp),
        ).start()

    loop(1, seq_count, send_second)
    second_others = gain_second.at[pl.ds(0, seq_count - 1)]
    pltpu.make_async_copy(second_others, second_others, gain_recv.at[1]).wait()
    gain = jnp.sum(gain_second[...], axis=0) / samples
    gain_out[0] = gain[:2]
    gain_out[1] = gain[2:]

    for copy in local_results:
        copy.wait()
    sent = (
        (image_in.at[pl.ds(0, 3), all_heads, my_rows], image_send.at[0]),
        (image_in.at[3, all_heads, my_rows], image_send.at[1]),
        (image_out.at[0, kept], image_back_send.at[0]),
        (image_proj_grad.at[:, 0, kept], image_back_send.at[1]),
        (image_out.at[0, given], image_back_recv.at[0]),
        (image_proj_grad.at[:, 0, given], image_back_recv.at[1]),
        (first_others, gain_send.at[0]),
        (second_others, gain_send.at[1]),
        (text_out, back_recv.at[0]),
        (text_proj_grad, back_recv.at[1]),
        (text_res.at[0, :, pl.ds(0, owner_count - 1)], back_send.at[0]),
        (text_res.at[pl.ds(1, 3), :, pl.ds(0, owner_count - 1)], back_send.at[1]),
    )
    for part, semaphore in sent:
        pltpu.make_async_copy(part, part, semaphore).wait()

    def sent_text(step):
        own = pl.ds(step * hps, hps)
        others = pl.ds(0, owner_count - 1)
        for i, part in enumerate((text_in.at[pl.ds(0, 3), own, others], text_in.at[3, own, others])):
            pltpu.make_async_copy(part, part, text_send.at[i, step]).wait()

    loop(0, steps, sent_text)


def per_device(sizes, text_proj, image_proj, text_grad, image_grad, text_lengths, norm_gains):
    dp_count, seq_count, _ = sizes
    _, _, head_count, text_group, size = text_proj.shape
    image_rows = image_proj.shape[3]
    heads = head_count // 2
    owners = seq_count * 2
    steps = heads // HEADS_PER_STEP
    bf16 = jnp.bfloat16
    anywhere = pl.BlockSpec(memory_space=pl.ANY)
    text_shape = (4, heads, owners, text_group, size)
    image_shape = (4, heads, 2 * image_rows, size)
    dma = pltpu.SemaphoreType.DMA
    total = owners * text_group + 2 * image_rows
    text_out, text_proj_grad, image_out, image_proj_grad, gain_grad = pl.pallas_call(
        functools.partial(kernel, sizes),
        out_shape=(
            jax.ShapeDtypeStruct(text_grad.shape, bf16),
            jax.ShapeDtypeStruct(text_proj.shape, bf16),
            jax.ShapeDtypeStruct(image_grad.shape, bf16),
            jax.ShapeDtypeStruct(image_proj.shape, bf16),
            jax.ShapeDtypeStruct(norm_gains.shape, jnp.float32),
        ),
        in_specs=[anywhere] * 4
        + [pl.BlockSpec(memory_space=pltpu.SMEM), pl.BlockSpec(memory_space=pltpu.VMEM)],
        out_specs=(anywhere,) * 4 + (pl.BlockSpec(memory_space=pltpu.VMEM),),
        scratch_shapes=[
            pltpu.VMEM(text_shape, bf16),
            pltpu.VMEM(image_shape, bf16),
            pltpu.VMEM(text_shape, bf16),
            pltpu.VMEM(image_shape, bf16),
            pltpu.VMEM((4, size), jnp.float32),
            pltpu.VMEM((2 * dp_count, 4, size), jnp.float32),
            pltpu.VMEM((4, size), jnp.float32),
            pltpu.VMEM((seq_count, 4, size), jnp.float32),
            dma((2, steps)),
            dma((2, steps)),
            dma((2,)),
            dma((4,)),
            dma((2,)),
            dma((2,)),
            dma((2,)),
            dma((4,)),
            dma((2,)),
            dma((2,)),
        ],
        compiler_params=pltpu.CompilerParams(
            collective_id=0, has_side_effects=True, vmem_limit_bytes=40 << 20
        ),
        cost_estimate=pl.CostEstimate(
            flops=heads * 12 * total * total * size,
            bytes_accessed=2 * 8 * heads * total * size * 2,
            transcendentals=heads * total * total,
        ),
    )(text_proj, text_grad, image_proj, image_grad, text_lengths, norm_gains)
    return text_out, image_out, text_proj_grad, image_proj_grad, gain_grad


def solution(mesh):
    dp_count, seq_count = mesh.shape["dp"], mesh.shape["seq"]
    text_proj = P(None, "dp", None, ("seq", "grp"), None)
    image_proj = P(None, ("dp", "seq"), None, "grp", None)
    text_grad = P("dp", None, ("seq", "grp"), None)
    image_grad = P(("dp", "seq"), None, "grp", None)

    def run(*args):
        sizes = (dp_count, seq_count, args[4].shape[0])
        return jax.shard_map(
            functools.partial(per_device, sizes),
            mesh=mesh,
            in_specs=(text_proj, image_proj, text_grad, image_grad, P(("dp", "seq")), P()),
            out_specs=(text_grad, image_grad, text_proj, image_proj, P()),
            check_vma=False,
        )(*args)

    return run
```

```python
import functools

import jax
import jax.numpy as jnp
from jax import lax
from jax.experimental import pallas as pl
from jax.experimental.pallas import tpu as pltpu
from jax.sharding import PartitionSpec as P

EPSILON = 1e-06
MASKED = -1e30
MESH_ID = pl.DeviceIdType.MESH
NZ = 4
HEADS_PER_STEP = 1
VMEM_LIMIT = 60 << 20
HELD = 3
TURN = 11
STRIDE = 29


def dot(a, b, contract_a, contract_b):
    return lax.dot_general(
        a, b, (((contract_a,), (contract_b,)), ((), ())), preferred_element_type=jnp.float32
    )


def unit_parts(raw):
    raw_vals = raw.astype(jnp.float32)
    inverse = lax.rsqrt(jnp.mean(raw_vals * raw_vals, axis=-1, keepdims=True) + EPSILON)
    return raw_vals * inverse, inverse


def attend_head(query_raw, key_raw, value, cotangent, bias, gains, text_rows):
    total, size = query_raw.shape
    factor = size**-0.5

    def gain_rows(c):
        return jnp.concatenate(
            [
                jnp.broadcast_to(gains[0, c][None, :], (text_rows, size)),
                jnp.broadcast_to(gains[1, c][None, :], (total - text_rows, size)),
            ],
            axis=0,
        )

    query_unit, query_inverse = unit_parts(query_raw)
    key_unit, key_inverse = unit_parts(key_raw)
    query_gain, key_gain = gain_rows(0), gain_rows(1)
    query = (query_unit * query_gain).astype(jnp.bfloat16)
    key = (key_unit * key_gain).astype(jnp.bfloat16)

    scores = jnp.where(bias < 0, MASKED, dot(query, key, 1, 1) * factor)
    exponent = jnp.exp(scores - jnp.max(scores, axis=-1, keepdims=True))
    probs = exponent * (1.0 / jnp.sum(exponent, axis=-1, keepdims=True))
    rounded = probs.astype(jnp.bfloat16)
    attention = dot(rounded, value, 1, 0).astype(jnp.bfloat16)
    grad_value = dot(rounded, cotangent, 0, 0).astype(jnp.bfloat16)
    grad_probs = dot(cotangent, value, 1, 1)
    row_delta = jnp.sum(probs * grad_probs, axis=-1, keepdims=True)
    grad_scores = (probs * (grad_probs - row_delta) * factor).astype(jnp.bfloat16)

    def raw_gradient(grad_normed, unit, inverse, gain):
        grad_normed = grad_normed.astype(jnp.bfloat16).astype(jnp.float32)
        term = grad_normed * unit
        text_part = jnp.sum(term[:text_rows], axis=0, keepdims=True)
        image_part = jnp.sum(term[text_rows:], axis=0, keepdims=True)
        mean = jnp.mean(term * gain, axis=-1, keepdims=True)
        grad_raw = inverse * (grad_normed * gain - unit * mean)
        return grad_raw.astype(jnp.bfloat16), text_part, image_part

    grad_query, query_text, query_image = raw_gradient(
        dot(grad_scores, key, 1, 0), query_unit, query_inverse, query_gain
    )
    grad_key, key_text, key_image = raw_gradient(
        dot(grad_scores, query, 0, 0), key_unit, key_inverse, key_gain
    )
    parts = jnp.concatenate([query_text, key_text, query_image, key_image], axis=0)
    return (attention, grad_query, grad_key, grad_value), parts


def kernel(
    sizes,
    text_proj,
    text_grad,
    image_proj,
    image_grad,
    length_any,
    gains_any,
    text_out,
    text_proj_grad,
    image_out,
    image_proj_grad,
    gain_out,
    text_in,
    image_in,
    text_res,
    image_res,
    gain_part,
    gain_first,
    gain_mid,
    gain_second,
    length,
    gains,
    text_send,
    text_recv,
    image_send,
    image_recv,
    back_send,
    back_recv,
    image_back_send,
    image_back_recv,
    gain_send,
    gain_recv,
    small_recv,
):
    dp_count, seq_count, samples = sizes
    rows_y = seq_count // NZ
    dp, seq, grp = lax.axis_index("dp"), lax.axis_index("seq"), lax.axis_index("grp")
    other = 1 - grp
    owner_count = seq_count * 2
    me = seq * 2 + grp
    heads = text_in.shape[1]
    text_rows = owner_count * text_in.shape[3]
    image_rows = image_proj.shape[3]
    hps = HEADS_PER_STEP
    steps = heads // hps
    held = min(HELD, steps - 1)

    way = 1 - 2 * grp

    def seq_peer(k):
        y = lax.rem(seq // NZ + way * (k // NZ) + rows_y, rows_y)
        z = lax.rem(lax.rem(seq, NZ) + way * lax.rem(k, NZ) + NZ, NZ)
        return y * NZ + z

    def peer(k):
        turned = lax.rem(k - 1 + seq * TURN, owner_count - 1) + 1
        place = lax.rem(turned * STRIDE, owner_count)
        return seq_peer(place // 2), lax.rem(grp + place, 2)

    def first_peer(k):
        return lax.rem(dp + k // 2, dp_count), lax.rem(grp + k, 2)

    def loop(low, high, body):
        def step(k, carry):
            body(k)
            return carry

        lax.fori_loop(low, high, step, 0)

    barrier = pltpu.get_barrier_semaphore()

    def greet(k):
        peer_seq, peer_grp = peer(k)
        pl.semaphore_signal(
            barrier, inc=1, device_id=(dp, peer_seq, peer_grp), device_id_type=MESH_ID
        )

    def greet_first(k):
        peer_dp, peer_grp = first_peer(k)
        pl.semaphore_signal(
            barrier, inc=1, device_id=(peer_dp, seq, peer_grp), device_id_type=MESH_ID
        )

    loop(1, owner_count, greet)
    loop(2, 2 * dp_count, greet_first)

    all_heads = pl.ds(0, heads)
    given = pl.ds(pl.multiple_of(other * heads, heads), heads)
    kept = pl.ds(pl.multiple_of(grp * heads, heads), heads)
    my_rows = pl.ds(pl.multiple_of(grp * image_rows, image_rows), image_rows)
    other_rows = pl.ds(pl.multiple_of(other * image_rows, image_rows), image_rows)
    local_images = (
        pltpu.make_async_copy(
            image_proj.at[:, 0, kept],
            image_in.at[pl.ds(0, 3), all_heads, my_rows],
            image_recv.at[2],
        ),
        pltpu.make_async_copy(
            image_grad.at[0, kept], image_in.at[3, all_heads, my_rows], image_recv.at[3]
        ),
    )
    for copy in local_images:
        copy.start()
    small = (
        pltpu.make_async_copy(length_any, length, small_recv.at[0]),
        pltpu.make_async_copy(gains_any, gains, small_recv.at[1]),
    )
    for copy in small:
        copy.start()

    def text_ends(step, peer_seq, peer_grp):
        own = pl.ds(step * hps, hps)
        theirs = pl.ds(peer_grp * heads + step * hps, hps)
        return (
            (text_proj.at[:, peer_seq, theirs], text_in.at[pl.ds(0, 3), own, me]),
            (text_grad.at[peer_seq, theirs], text_in.at[3, own, me]),
        )

    def text_stays(step):
        for i, (src, dst) in enumerate(text_ends(step, seq, grp)):
            pltpu.make_async_copy(src, dst, text_recv.at[i, step]).start()

    loop(0, steps, text_stays)
    gain_part[...] = jnp.zeros_like(gain_part)
    pl.semaphore_wait(barrier, owner_count - 1 + 2 * dp_count - 2)

    def remote(src, dst, send, recv, target):
        return pltpu.make_async_remote_copy(
            src_ref=src,
            dst_ref=dst,
            send_sem=send,
            recv_sem=recv,
            device_id=target,
            device_id_type=MESH_ID,
        )

    partner = (dp, seq, other)
    remote(
        image_proj.at[:, 0, given],
        image_in.at[pl.ds(0, 3), all_heads, my_rows],
        image_send.at[0],
        image_recv.at[0],
        partner,
    ).start()
    remote(
        image_grad.at[0, given],
        image_in.at[3, all_heads, my_rows],
        image_send.at[1],
        image_recv.at[1],
        partner,
    ).start()
    def text_step(step):
        def send(k):
            peer_seq, peer_grp = peer(k)
            for i, (src, dst) in enumerate(text_ends(step, peer_seq, peer_grp)):
                remote(
                    src,
                    dst,
                    text_send.at[i, step],
                    text_recv.at[i, step],
                    (dp, peer_seq, peer_grp),
                ).start()

        loop(1, owner_count, send)

    loop(0, steps, text_step)

    for copy in local_images + small:
        copy.wait()
    for i, part in enumerate((image_in.at[pl.ds(0, 3), all_heads, other_rows], image_in.at[3, all_heads, other_rows])):
        pltpu.make_async_copy(part, part, image_recv.at[i]).wait()

    total = text_rows + 2 * image_rows
    place = lax.broadcasted_iota(jnp.int32, (1, total), 1)
    bias = jnp.where((place >= text_rows) | (place < length[0]), 0.0, -1.0)

    first_me = dp * 2 + grp
    first_others = gain_first.at[pl.ds(0, 2 * dp_count - 1)]
    second_others = gain_second.at[pl.ds(0, seq_count - 1)]

    def gain_hop_one():
        gain_first[first_me] = gain_part[...]

        def send_first(k):
            peer_dp, peer_grp = first_peer(k)
            remote(
                gain_part,
                gain_first.at[first_me],
                gain_send.at[0],
                gain_recv.at[0],
                (peer_dp, seq, peer_grp),
            ).start()

        loop(1, 2 * dp_count, send_first)

    def gain_hop_two():
        pltpu.make_async_copy(first_others, first_others, gain_recv.at[0]).wait()
        mid = jnp.sum(gain_first[...], axis=0)
        gain_mid[...] = mid
        gain_second[seq] = mid

        def send_second(k):
            remote(
                gain_mid,
                gain_second.at[seq],
                gain_send.at[1],
                gain_recv.at[1],
                (dp, seq_peer(k), grp),
            ).start()

        loop(1, seq_count, send_second)

    def give_back(step):
        own = pl.ds(step * hps, hps)
        there = pl.ds(grp * heads + step * hps, hps)

        def back_ends(owner):
            return (
                (text_res.at[0, own, owner], text_out.at[seq, there]),
                (text_res.at[pl.ds(1, 3), own, owner], text_proj_grad.at[:, seq, there]),
            )

        def send_back(k):
            peer_seq, peer_grp = peer(k)
            for i, (src, dst) in enumerate(back_ends(peer_seq * 2 + peer_grp)):
                remote(
                    src, dst, back_send.at[i], back_recv.at[i], (dp, peer_seq, peer_grp)
                ).start()

        loop(1, owner_count, send_back)
        for i, (src, dst) in enumerate(back_ends(me)):
            pltpu.make_async_copy(src, dst, back_recv.at[i]).start()

    def work(step):
        own = pl.ds(step * hps, hps)
        for i, part in enumerate((text_in.at[pl.ds(0, 3), own], text_in.at[3, own])):
            pltpu.make_async_copy(part, part, text_recv.at[i, step]).wait()
        for j in range(hps):
            head = step * hps + j
            rows = [
                jnp.concatenate(
                    [
                        text_in[c, head].reshape(text_rows, text_in.shape[-1]),
                        image_in[c, head],
                    ],
                    axis=0,
                )
                for c in range(4)
            ]
            results, parts = attend_head(*rows, bias, gains, text_rows)
            gain_part[...] += parts
            for c, result in enumerate(results):
                text_res[c, head] = result[:text_rows].reshape(text_res.shape[2:])
                image_res[c, head] = result[text_rows:]
        pl.when(step < held)(lambda: give_back(step))

    loop(0, steps, work)
    gain_hop_one()
    loop(held, steps - 1, give_back)
    gain_hop_two()
    loop(steps - 1, steps, give_back)

    remote(
        image_res.at[0, all_heads, other_rows],
        image_out.at[0, kept],
        image_back_send.at[0],
        image_back_recv.at[0],
        partner,
    ).start()
    remote(
        image_res.at[pl.ds(1, 3), all_heads, other_rows],
        image_proj_grad.at[:, 0, kept],
        image_back_send.at[1],
        image_back_recv.at[1],
        partner,
    ).start()
    local_results = (
        pltpu.make_async_copy(
            image_res.at[0, all_heads, my_rows], image_out.at[0, kept], image_back_recv.at[2]
        ),
        pltpu.make_async_copy(
            image_res.at[pl.ds(1, 3), all_heads, my_rows],
            image_proj_grad.at[:, 0, kept],
            image_back_recv.at[3],
        ),
    )
    for copy in local_results:
        copy.start()

    pltpu.make_async_copy(second_others, second_others, gain_recv.at[1]).wait()
    gain = jnp.sum(gain_second[...], axis=0) / samples
    gain_out[0] = gain[:2]
    gain_out[1] = gain[2:]

    for copy in local_results:
        copy.wait()
    sent = (
        (image_in.at[pl.ds(0, 3), all_heads, my_rows], image_send.at[0]),
        (image_in.at[3, all_heads, my_rows], image_send.at[1]),
        (image_out.at[0, kept], image_back_send.at[0]),
        (image_proj_grad.at[:, 0, kept], image_back_send.at[1]),
        (image_out.at[0, given], image_back_recv.at[0]),
        (image_proj_grad.at[:, 0, given], image_back_recv.at[1]),
        (first_others, gain_send.at[0]),
        (second_others, gain_send.at[1]),
        (text_out, back_recv.at[0]),
        (text_proj_grad, back_recv.at[1]),
        (text_res.at[0, :, pl.ds(0, owner_count - 1)], back_send.at[0]),
        (text_res.at[pl.ds(1, 3), :, pl.ds(0, owner_count - 1)], back_send.at[1]),
    )
    for part, semaphore in sent:
        pltpu.make_async_copy(part, part, semaphore).wait()

    def sent_text(step):
        own = pl.ds(step * hps, hps)
        others = pl.ds(0, owner_count - 1)
        for i, part in enumerate((text_in.at[pl.ds(0, 3), own, others], text_in.at[3, own, others])):
            pltpu.make_async_copy(part, part, text_send.at[i, step]).wait()

    loop(0, steps, sent_text)


def put_out(count, *refs):
    results, outs, held = refs[:count], refs[count : 2 * count], refs[2 * count : 3 * count]
    semaphores = refs[-1]
    reads = [
        pltpu.make_async_copy(results[i], held[i], semaphores.at[0, i]) for i in range(count)
    ]
    writes = [pltpu.make_async_copy(held[i], outs[i], semaphores.at[1, i]) for i in range(count)]
    for copy in reads:
        copy.start()
    for read, write in zip(reads, writes):
        read.wait()
        write.start()
    for copy in writes:
        copy.wait()


def per_device(sizes, text_proj, image_proj, text_grad, image_grad, text_lengths, norm_gains):
    dp_count, seq_count, _ = sizes
    _, _, head_count, text_group, size = text_proj.shape
    image_rows = image_proj.shape[3]
    heads = head_count // 2
    owners = seq_count * 2
    steps = heads // HEADS_PER_STEP
    bf16 = jnp.bfloat16
    anywhere = pl.BlockSpec(memory_space=pl.ANY)
    text_shape = (4, heads, owners, text_group, size)
    image_shape = (4, heads, 2 * image_rows, size)
    dma = pltpu.SemaphoreType.DMA
    total = owners * text_group + 2 * image_rows
    results = pl.pallas_call(
        functools.partial(kernel, sizes),
        out_shape=(
            jax.ShapeDtypeStruct(text_grad.shape, bf16),
            jax.ShapeDtypeStruct(text_proj.shape, bf16),
            jax.ShapeDtypeStruct(image_grad.shape, bf16),
            jax.ShapeDtypeStruct(image_proj.shape, bf16),
            jax.ShapeDtypeStruct(norm_gains.shape, jnp.float32),
        ),
        in_specs=[anywhere] * 6,
        out_specs=(anywhere,) * 4 + (pl.BlockSpec(memory_space=pltpu.VMEM),),
        scratch_shapes=[
            pltpu.VMEM(text_shape, bf16),
            pltpu.VMEM(image_shape, bf16),
            pltpu.VMEM(text_shape, bf16),
            pltpu.VMEM(image_shape, bf16),
            pltpu.VMEM((4, size), jnp.float32),
            pltpu.VMEM((2 * dp_count, 4, size), jnp.float32),
            pltpu.VMEM((4, size), jnp.float32),
            pltpu.VMEM((seq_count, 4, size), jnp.float32),
            pltpu.SMEM((1,), jnp.int32),
            pltpu.VMEM(norm_gains.shape, jnp.float32),
            dma((2, steps)),
            dma((2, steps)),
            dma((2,)),
            dma((4,)),
            dma((2,)),
            dma((2,)),
            dma((2,)),
            dma((4,)),
            dma((2,)),
            dma((2,)),
            dma((2,)),
        ],
        compiler_params=pltpu.CompilerParams(
            collective_id=0, has_side_effects=True, vmem_limit_bytes=VMEM_LIMIT
        ),
        cost_estimate=pl.CostEstimate(
            flops=heads * 12 * total * total * size,
            bytes_accessed=2 * 8 * heads * total * size * 2,
            transcendentals=heads * total * total,
        ),
    )(text_proj, text_grad, image_proj, image_grad, text_lengths, norm_gains)
    text_out, text_proj_grad, image_out, image_proj_grad, gain_grad = pl.pallas_call(
        functools.partial(put_out, len(results)),
        out_shape=tuple(jax.ShapeDtypeStruct(r.shape, r.dtype) for r in results),
        in_specs=[anywhere] * len(results),
        out_specs=(anywhere,) * len(results),
        scratch_shapes=[pltpu.VMEM(r.shape, r.dtype) for r in results] + [dma((2, len(results)))],
        compiler_params=pltpu.CompilerParams(vmem_limit_bytes=VMEM_LIMIT),
    )(*results)
    return text_out, image_out, text_proj_grad, image_proj_grad, gain_grad


def solution(mesh):
    dp_count, seq_count = mesh.shape["dp"], mesh.shape["seq"]
    text_proj = P(None, "dp", None, ("seq", "grp"), None)
    image_proj = P(None, ("dp", "seq"), None, "grp", None)
    text_grad = P("dp", None, ("seq", "grp"), None)
    image_grad = P(("dp", "seq"), None, "grp", None)

    def run(*args):
        sizes = (dp_count, seq_count, args[4].shape[0])
        return jax.shard_map(
            functools.partial(per_device, sizes),
            mesh=mesh,
            in_specs=(text_proj, image_proj, text_grad, image_grad, P(("dp", "seq")), P()),
            out_specs=(text_grad, image_grad, text_proj, image_proj, P()),
            check_vma=False,
        )(*args)

    return run
```

```python
import functools

import jax
import jax.numpy as jnp
from jax import lax
from jax.experimental import pallas as pl
from jax.experimental.pallas import tpu as pltpu
from jax.sharding import PartitionSpec as P

EPSILON = 1e-06
MASKED = -1e30
MESH_ID = pl.DeviceIdType.MESH
NZ = 4
HEADS_PER_STEP = 2
VMEM_LIMIT = 60 << 20
HELD = 1
THIRD_AFTER = 40
TURN = 11
STRIDE = 29


def dot(a, b, contract_a, contract_b):
    return lax.dot_general(
        a, b, (((contract_a,), (contract_b,)), ((), ())), preferred_element_type=jnp.float32
    )


def unit_parts(raw):
    raw_vals = raw.astype(jnp.float32)
    inverse = lax.rsqrt(jnp.mean(raw_vals * raw_vals, axis=-1, keepdims=True) + EPSILON)
    return raw_vals * inverse, inverse


def attend_head(query_raw, key_raw, value, cotangent, bias, gains, text_rows):
    total, size = query_raw.shape
    factor = size**-0.5

    def gain_rows(c):
        return jnp.concatenate(
            [
                jnp.broadcast_to(gains[0, c][None, :], (text_rows, size)),
                jnp.broadcast_to(gains[1, c][None, :], (total - text_rows, size)),
            ],
            axis=0,
        )

    query_unit, query_inverse = unit_parts(query_raw)
    key_unit, key_inverse = unit_parts(key_raw)
    query_gain, key_gain = gain_rows(0), gain_rows(1)
    query = (query_unit * query_gain).astype(jnp.bfloat16)
    key = (key_unit * key_gain).astype(jnp.bfloat16)

    scores = jnp.where(bias < 0, MASKED, dot(query, key, 1, 1) * factor)
    exponent = jnp.exp(scores - jnp.max(scores, axis=-1, keepdims=True))
    probs = exponent * (1.0 / jnp.sum(exponent, axis=-1, keepdims=True))
    rounded = probs.astype(jnp.bfloat16)
    attention = dot(rounded, value, 1, 0).astype(jnp.bfloat16)
    grad_value = dot(rounded, cotangent, 0, 0).astype(jnp.bfloat16)
    grad_probs = dot(cotangent, value, 1, 1)
    row_delta = jnp.sum(probs * grad_probs, axis=-1, keepdims=True)
    grad_scores = (probs * (grad_probs - row_delta) * factor).astype(jnp.bfloat16)

    def raw_gradient(grad_normed, unit, inverse, gain):
        grad_normed = grad_normed.astype(jnp.bfloat16).astype(jnp.float32)
        term = grad_normed * unit
        text_part = jnp.sum(term[:text_rows], axis=0, keepdims=True)
        image_part = jnp.sum(term[text_rows:], axis=0, keepdims=True)
        mean = jnp.mean(term * gain, axis=-1, keepdims=True)
        grad_raw = inverse * (grad_normed * gain - unit * mean)
        return grad_raw.astype(jnp.bfloat16), text_part, image_part

    grad_query, query_text, query_image = raw_gradient(
        dot(grad_scores, key, 1, 0), query_unit, query_inverse, query_gain
    )
    grad_key, key_text, key_image = raw_gradient(
        dot(grad_scores, query, 0, 0), key_unit, key_inverse, key_gain
    )
    parts = jnp.concatenate([query_text, key_text, query_image, key_image], axis=0)
    return (attention, grad_query, grad_key, grad_value), parts


def kernel(
    sizes,
    text_proj,
    text_grad,
    image_proj,
    image_grad,
    length_any,
    gains_any,
    text_out,
    text_proj_grad,
    image_out,
    image_proj_grad,
    gain_out,
    text_in,
    image_in,
    text_res,
    image_res,
    gain_part,
    gain_first,
    gain_mid,
    gain_second,
    gain_late,
    gain_third,
    length,
    gains,
    text_send,
    text_recv,
    image_send,
    image_recv,
    back_send,
    back_recv,
    image_back_send,
    image_back_recv,
    gain_send,
    gain_recv,
    small_recv,
):
    dp_count, seq_count, samples = sizes
    rows_y = seq_count // NZ
    dp, seq, grp = lax.axis_index("dp"), lax.axis_index("seq"), lax.axis_index("grp")
    other = 1 - grp
    owner_count = seq_count * 2
    me = seq * 2 + grp
    heads = text_in.shape[1]
    text_rows = owner_count * text_in.shape[3]
    image_rows = image_proj.shape[3]
    hps = HEADS_PER_STEP
    steps = heads // hps
    held = min(HELD, steps - 1)

    way = 1 - 2 * grp

    def seq_peer(k):
        y = lax.rem(seq // NZ + way * (k // NZ) + rows_y, rows_y)
        z = lax.rem(lax.rem(seq, NZ) + way * lax.rem(k, NZ) + NZ, NZ)
        return y * NZ + z

    def peer(k):
        turned = lax.rem(k - 1 + seq * TURN, owner_count - 1) + 1
        place = lax.rem(turned * STRIDE, owner_count)
        return seq_peer(place // 2), lax.rem(grp + place, 2)

    def first_peer(k):
        return lax.rem(dp + k // 2, dp_count), lax.rem(grp + k, 2)

    def loop(low, high, body):
        def step(k, carry):
            body(k)
            return carry

        lax.fori_loop(low, high, step, 0)

    barrier = pltpu.get_barrier_semaphore()

    def greet(k):
        peer_seq, peer_grp = peer(k)
        pl.semaphore_signal(
            barrier, inc=1, device_id=(dp, peer_seq, peer_grp), device_id_type=MESH_ID
        )

    def greet_first(k):
        peer_dp, peer_grp = first_peer(k)
        pl.semaphore_signal(
            barrier, inc=1, device_id=(peer_dp, seq, peer_grp), device_id_type=MESH_ID
        )

    loop(1, owner_count, greet)
    loop(2, 2 * dp_count, greet_first)

    all_heads = pl.ds(0, heads)
    given = pl.ds(pl.multiple_of(other * heads, heads), heads)
    kept = pl.ds(pl.multiple_of(grp * heads, heads), heads)
    my_rows = pl.ds(pl.multiple_of(grp * image_rows, image_rows), image_rows)
    other_rows = pl.ds(pl.multiple_of(other * image_rows, image_rows), image_rows)
    local_images = (
        pltpu.make_async_copy(
            image_proj.at[:, 0, kept],
            image_in.at[pl.ds(0, 3), all_heads, my_rows],
            image_recv.at[2],
        ),
        pltpu.make_async_copy(
            image_grad.at[0, kept], image_in.at[3, all_heads, my_rows], image_recv.at[3]
        ),
    )
    for copy in local_images:
        copy.start()
    small = (
        pltpu.make_async_copy(length_any, length, small_recv.at[0]),
        pltpu.make_async_copy(gains_any, gains, small_recv.at[1]),
    )
    for copy in small:
        copy.start()

    def text_ends(step, peer_seq, peer_grp):
        own = pl.ds(step * hps, hps)
        theirs = pl.ds(peer_grp * heads + step * hps, hps)
        return (
            (text_proj.at[:, peer_seq, theirs], text_in.at[pl.ds(0, 3), own, me]),
            (text_grad.at[peer_seq, theirs], text_in.at[3, own, me]),
        )

    def text_stays(step):
        for i, (src, dst) in enumerate(text_ends(step, seq, grp)):
            pltpu.make_async_copy(src, dst, text_recv.at[i, step]).start()

    loop(0, steps, text_stays)
    gain_part[...] = jnp.zeros_like(gain_part)
    pl.semaphore_wait(barrier, owner_count - 1 + 2 * dp_count - 2)

    def remote(src, dst, send, recv, target):
        return pltpu.make_async_remote_copy(
            src_ref=src,
            dst_ref=dst,
            send_sem=send,
            recv_sem=recv,
            device_id=target,
            device_id_type=MESH_ID,
        )

    partner = (dp, seq, other)
    remote(
        image_proj.at[:, 0, given],
        image_in.at[pl.ds(0, 3), all_heads, my_rows],
        image_send.at[0],
        image_recv.at[0],
        partner,
    ).start()
    remote(
        image_grad.at[0, given],
        image_in.at[3, all_heads, my_rows],
        image_send.at[1],
        image_recv.at[1],
        partner,
    ).start()
    def text_step(step):
        def send(k):
            peer_seq, peer_grp = peer(k)
            for i, (src, dst) in enumerate(text_ends(step, peer_seq, peer_grp)):
                remote(
                    src,
                    dst,
                    text_send.at[i, step],
                    text_recv.at[i, step],
                    (dp, peer_seq, peer_grp),
                ).start()

        loop(1, owner_count, send)

    loop(0, steps, text_step)

    for copy in local_images + small:
        copy.wait()
    for i, part in enumerate((image_in.at[pl.ds(0, 3), all_heads, other_rows], image_in.at[3, all_heads, other_rows])):
        pltpu.make_async_copy(part, part, image_recv.at[i]).wait()

    total = text_rows + 2 * image_rows
    place = lax.broadcasted_iota(jnp.int32, (1, total), 1)
    bias = jnp.where((place >= text_rows) | (place < length[0]), 0.0, -1.0)

    first_me = dp * 2 + grp
    first_others = gain_first.at[pl.ds(0, 2 * dp_count - 1)]
    second_others = gain_second.at[pl.ds(0, rows_y - 1)]
    third_others = gain_third.at[pl.ds(0, NZ - 1)]
    my_y, my_z = seq // NZ, lax.rem(seq, NZ)

    def gain_hop_one():
        gain_first[first_me] = gain_part[...]

        def send_first(k):
            peer_dp, peer_grp = first_peer(k)
            remote(
                gain_part,
                gain_first.at[first_me],
                gain_send.at[0],
                gain_recv.at[0],
                (peer_dp, seq, peer_grp),
            ).start()

        loop(1, 2 * dp_count, send_first)

    def gain_hop_two():
        pltpu.make_async_copy(first_others, first_others, gain_recv.at[0]).wait()
        mid = jnp.sum(gain_first[...], axis=0)
        gain_mid[...] = mid
        gain_second[my_y] = mid

        def send_second(k):
            remote(
                gain_mid,
                gain_second.at[my_y],
                gain_send.at[1],
                gain_recv.at[1],
                (dp, seq_peer(k * NZ), grp),
            ).start()

        loop(1, rows_y, send_second)

    def gain_hop_three():
        pltpu.make_async_copy(second_others, second_others, gain_recv.at[1]).wait()
        late = jnp.sum(gain_second[...], axis=0)
        gain_late[...] = late
        gain_third[my_z] = late

        def send_third(k):
            remote(
                gain_late,
                gain_third.at[my_z],
                gain_send.at[2],
                gain_recv.at[2],
                (dp, seq_peer(k), grp),
            ).start()

        loop(1, NZ, send_third)

    def give_back(step, low=1, high=owner_count):
        own = pl.ds(step * hps, hps)
        there = pl.ds(grp * heads + step * hps, hps)

        def back_ends(owner):
            return (
                (text_res.at[0, own, owner], text_out.at[seq, there]),
                (text_res.at[pl.ds(1, 3), own, owner], text_proj_grad.at[:, seq, there]),
            )

        def send_back(k):
            peer_seq, peer_grp = peer(k)
            for i, (src, dst) in enumerate(back_ends(peer_seq * 2 + peer_grp)):
                remote(
                    src, dst, back_send.at[i], back_recv.at[i], (dp, peer_seq, peer_grp)
                ).start()

        loop(low, high, send_back)
        if low == 1:
            for i, (src, dst) in enumerate(back_ends(me)):
                pltpu.make_async_copy(src, dst, back_recv.at[i]).start()

    def work(step):
        own = pl.ds(step * hps, hps)
        for i, part in enumerate((text_in.at[pl.ds(0, 3), own], text_in.at[3, own])):
            pltpu.make_async_copy(part, part, text_recv.at[i, step]).wait()
        for j in range(hps):
            head = step * hps + j
            rows = [
                jnp.concatenate(
                    [
                        text_in[c, head].reshape(text_rows, text_in.shape[-1]),
                        image_in[c, head],
                    ],
                    axis=0,
                )
                for c in range(4)
            ]
            results, parts = attend_head(*rows, bias, gains, text_rows)
            gain_part[...] += parts
            for c, result in enumerate(results):
                text_res[c, head] = result[:text_rows].reshape(text_res.shape[2:])
                image_res[c, head] = result[text_rows:]
        pl.when(step < held)(lambda: give_back(step))

    loop(0, steps, work)
    gain_hop_one()
    loop(held, steps - 1, give_back)
    gain_hop_two()
    third_after = min(THIRD_AFTER, owner_count)
    give_back(steps - 1, 1, third_after)
    gain_hop_three()
    give_back(steps - 1, third_after, owner_count)

    remote(
        image_res.at[0, all_heads, other_rows],
        image_out.at[0, kept],
        image_back_send.at[0],
        image_back_recv.at[0],
        partner,
    ).start()
    remote(
        image_res.at[pl.ds(1, 3), all_heads, other_rows],
        image_proj_grad.at[:, 0, kept],
        image_back_send.at[1],
        image_back_recv.at[1],
        partner,
    ).start()
    local_results = (
        pltpu.make_async_copy(
            image_res.at[0, all_heads, my_rows], image_out.at[0, kept], image_back_recv.at[2]
        ),
        pltpu.make_async_copy(
            image_res.at[pl.ds(1, 3), all_heads, my_rows],
            image_proj_grad.at[:, 0, kept],
            image_back_recv.at[3],
        ),
    )
    for copy in local_results:
        copy.start()

    pltpu.make_async_copy(third_others, third_others, gain_recv.at[2]).wait()
    gain = jnp.sum(gain_third[...], axis=0) / samples
    gain_out[0] = gain[:2]
    gain_out[1] = gain[2:]

    for copy in local_results:
        copy.wait()
    sent = (
        (image_in.at[pl.ds(0, 3), all_heads, my_rows], image_send.at[0]),
        (image_in.at[3, all_heads, my_rows], image_send.at[1]),
        (image_out.at[0, kept], image_back_send.at[0]),
        (image_proj_grad.at[:, 0, kept], image_back_send.at[1]),
        (image_out.at[0, given], image_back_recv.at[0]),
        (image_proj_grad.at[:, 0, given], image_back_recv.at[1]),
        (first_others, gain_send.at[0]),
        (second_others, gain_send.at[1]),
        (third_others, gain_send.at[2]),
        (text_out, back_recv.at[0]),
        (text_proj_grad, back_recv.at[1]),
        (text_res.at[0, :, pl.ds(0, owner_count - 1)], back_send.at[0]),
        (text_res.at[pl.ds(1, 3), :, pl.ds(0, owner_count - 1)], back_send.at[1]),
    )
    for part, semaphore in sent:
        pltpu.make_async_copy(part, part, semaphore).wait()

    def sent_text(step):
        own = pl.ds(step * hps, hps)
        others = pl.ds(0, owner_count - 1)
        for i, part in enumerate((text_in.at[pl.ds(0, 3), own, others], text_in.at[3, own, others])):
            pltpu.make_async_copy(part, part, text_send.at[i, step]).wait()

    loop(0, steps, sent_text)


def put_out(count, *refs):
    results, outs, held = refs[:count], refs[count : 2 * count], refs[2 * count : 3 * count]
    semaphores = refs[-1]
    reads = [
        pltpu.make_async_copy(results[i], held[i], semaphores.at[0, i]) for i in range(count)
    ]
    writes = [pltpu.make_async_copy(held[i], outs[i], semaphores.at[1, i]) for i in range(count)]
    for copy in reads:
        copy.start()
    for read, write in zip(reads, writes):
        read.wait()
        write.start()
    for copy in writes:
        copy.wait()


def per_device(sizes, text_proj, image_proj, text_grad, image_grad, text_lengths, norm_gains):
    dp_count, seq_count, _ = sizes
    _, _, head_count, text_group, size = text_proj.shape
    image_rows = image_proj.shape[3]
    heads = head_count // 2
    owners = seq_count * 2
    steps = heads // HEADS_PER_STEP
    bf16 = jnp.bfloat16
    anywhere = pl.BlockSpec(memory_space=pl.ANY)
    text_shape = (4, heads, owners, text_group, size)
    image_shape = (4, heads, 2 * image_rows, size)
    dma = pltpu.SemaphoreType.DMA
    total = owners * text_group + 2 * image_rows
    results = pl.pallas_call(
        functools.partial(kernel, sizes),
        out_shape=(
            jax.ShapeDtypeStruct(text_grad.shape, bf16),
            jax.ShapeDtypeStruct(text_proj.shape, bf16),
            jax.ShapeDtypeStruct(image_grad.shape, bf16),
            jax.ShapeDtypeStruct(image_proj.shape, bf16),
            jax.ShapeDtypeStruct(norm_gains.shape, jnp.float32),
        ),
        in_specs=[anywhere] * 6,
        out_specs=(anywhere,) * 4 + (pl.BlockSpec(memory_space=pltpu.VMEM),),
        scratch_shapes=[
            pltpu.VMEM(text_shape, bf16),
            pltpu.VMEM(image_shape, bf16),
            pltpu.VMEM(text_shape, bf16),
            pltpu.VMEM(image_shape, bf16),
            pltpu.VMEM((4, size), jnp.float32),
            pltpu.VMEM((2 * dp_count, 4, size), jnp.float32),
            pltpu.VMEM((4, size), jnp.float32),
            pltpu.VMEM((seq_count // NZ, 4, size), jnp.float32),
            pltpu.VMEM((4, size), jnp.float32),
            pltpu.VMEM((NZ, 4, size), jnp.float32),
            pltpu.SMEM((1,), jnp.int32),
            pltpu.VMEM(norm_gains.shape, jnp.float32),
            dma((2, steps)),
            dma((2, steps)),
            dma((2,)),
            dma((4,)),
            dma((2,)),
            dma((2,)),
            dma((2,)),
            dma((4,)),
            dma((3,)),
            dma((3,)),
            dma((2,)),
        ],
        compiler_params=pltpu.CompilerParams(
            collective_id=0, has_side_effects=True, vmem_limit_bytes=VMEM_LIMIT
        ),
        cost_estimate=pl.CostEstimate(
            flops=heads * 12 * total * total * size,
            bytes_accessed=2 * 8 * heads * total * size * 2,
            transcendentals=heads * total * total,
        ),
    )(text_proj, text_grad, image_proj, image_grad, text_lengths, norm_gains)
    text_out, text_proj_grad, image_out, image_proj_grad, gain_grad = pl.pallas_call(
        functools.partial(put_out, len(results)),
        out_shape=tuple(jax.ShapeDtypeStruct(r.shape, r.dtype) for r in results),
        in_specs=[anywhere] * len(results),
        out_specs=(anywhere,) * len(results),
        scratch_shapes=[pltpu.VMEM(r.shape, r.dtype) for r in results] + [dma((2, len(results)))],
        compiler_params=pltpu.CompilerParams(vmem_limit_bytes=VMEM_LIMIT),
    )(*results)
    return text_out, image_out, text_proj_grad, image_proj_grad, gain_grad


def solution(mesh):
    dp_count, seq_count = mesh.shape["dp"], mesh.shape["seq"]
    text_proj = P(None, "dp", None, ("seq", "grp"), None)
    image_proj = P(None, ("dp", "seq"), None, "grp", None)
    text_grad = P("dp", None, ("seq", "grp"), None)
    image_grad = P(("dp", "seq"), None, "grp", None)

    def run(*args):
        sizes = (dp_count, seq_count, args[4].shape[0])
        return jax.shard_map(
            functools.partial(per_device, sizes),
            mesh=mesh,
            in_specs=(text_proj, image_proj, text_grad, image_grad, P(("dp", "seq")), P()),
            out_specs=(text_grad, image_grad, text_proj, image_proj, P()),
            check_vma=False,
        )(*args)

    return run
```

```python
import functools

import jax
import jax.numpy as jnp
from jax import lax
from jax.experimental import pallas as pl
from jax.experimental.pallas import tpu as pltpu
from jax.sharding import PartitionSpec as P

EPSILON = 1e-06
MASKED = -1e30
MESH_ID = pl.DeviceIdType.MESH
NZ = 4
HEADS_PER_STEP = 2
VMEM_LIMIT = 60 << 20
PIECES = 4
HELD = 1
THIRD_AFTER = 40
TURN = 11
STRIDE = 29


def dot(a, b, contract_a, contract_b):
    return lax.dot_general(
        a, b, (((contract_a,), (contract_b,)), ((), ())), preferred_element_type=jnp.float32
    )


def unit_parts(raw):
    raw_vals = raw.astype(jnp.float32)
    inverse = lax.rsqrt(jnp.mean(raw_vals * raw_vals, axis=-1, keepdims=True) + EPSILON)
    return raw_vals * inverse, inverse


def attend_head(query_raw, key_raw, value, cotangent, bias, gains, text_rows):
    total, size = query_raw.shape
    factor = size**-0.5

    def gain_rows(c):
        return jnp.concatenate(
            [
                jnp.broadcast_to(gains[0, c][None, :], (text_rows, size)),
                jnp.broadcast_to(gains[1, c][None, :], (total - text_rows, size)),
            ],
            axis=0,
        )

    query_unit, query_inverse = unit_parts(query_raw)
    key_unit, key_inverse = unit_parts(key_raw)
    query_gain, key_gain = gain_rows(0), gain_rows(1)
    query = (query_unit * query_gain).astype(jnp.bfloat16)
    key = (key_unit * key_gain).astype(jnp.bfloat16)

    scores = jnp.where(bias < 0, MASKED, dot(query, key, 1, 1) * factor)
    exponent = jnp.exp(scores - jnp.max(scores, axis=-1, keepdims=True))
    probs = exponent * (1.0 / jnp.sum(exponent, axis=-1, keepdims=True))
    rounded = probs.astype(jnp.bfloat16)
    attention = dot(rounded, value, 1, 0).astype(jnp.bfloat16)
    grad_value = dot(rounded, cotangent, 0, 0).astype(jnp.bfloat16)
    grad_probs = dot(cotangent, value, 1, 1)
    row_delta = jnp.sum(probs * grad_probs, axis=-1, keepdims=True)
    grad_scores = (probs * (grad_probs - row_delta) * factor).astype(jnp.bfloat16)

    def raw_gradient(grad_normed, unit, inverse, gain):
        grad_normed = grad_normed.astype(jnp.bfloat16).astype(jnp.float32)
        term = grad_normed * unit
        text_part = jnp.sum(term[:text_rows], axis=0, keepdims=True)
        image_part = jnp.sum(term[text_rows:], axis=0, keepdims=True)
        mean = jnp.mean(term * gain, axis=-1, keepdims=True)
        grad_raw = inverse * (grad_normed * gain - unit * mean)
        return grad_raw.astype(jnp.bfloat16), text_part, image_part

    grad_query, query_text, query_image = raw_gradient(
        dot(grad_scores, key, 1, 0), query_unit, query_inverse, query_gain
    )
    grad_key, key_text, key_image = raw_gradient(
        dot(grad_scores, query, 0, 0), key_unit, key_inverse, key_gain
    )
    parts = jnp.concatenate([query_text, key_text, query_image, key_image], axis=0)
    return (attention, grad_query, grad_key, grad_value), parts


def kernel(
    sizes,
    text_proj,
    text_grad,
    image_proj,
    image_grad,
    length_any,
    gains_any,
    text_out,
    text_proj_grad,
    image_out,
    image_proj_grad,
    gain_out,
    text_in,
    image_in,
    text_res,
    image_res,
    gain_part,
    gain_first,
    gain_mid,
    gain_second,
    gain_late,
    gain_third,
    length,
    gains,
    text_send,
    text_recv,
    image_send,
    image_recv,
    back_send,
    back_recv,
    image_back_send,
    image_back_recv,
    gain_send,
    gain_recv,
    small_recv,
):
    dp_count, seq_count, samples = sizes
    rows_y = seq_count // NZ
    dp, seq, grp = lax.axis_index("dp"), lax.axis_index("seq"), lax.axis_index("grp")
    other = 1 - grp
    owner_count = seq_count * 2
    me = seq * 2 + grp
    heads = text_in.shape[1]
    text_rows = owner_count * text_in.shape[3]
    image_rows = image_proj.shape[3]
    hps = HEADS_PER_STEP
    steps = heads // hps
    held = min(HELD, steps - 1)

    way = 1 - 2 * grp

    def seq_peer(k):
        y = lax.rem(seq // NZ + way * (k // NZ) + rows_y, rows_y)
        z = lax.rem(lax.rem(seq, NZ) + way * lax.rem(k, NZ) + NZ, NZ)
        return y * NZ + z

    def peer(k):
        turned = lax.rem(k - 1 + seq * TURN, owner_count - 1) + 1
        place = lax.rem(turned * STRIDE, owner_count)
        return seq_peer(place // 2), lax.rem(grp + place, 2)

    def first_peer(k):
        return lax.rem(dp + k // 2, dp_count), lax.rem(grp + k, 2)

    def loop(low, high, body):
        def step(k, carry):
            body(k)
            return carry

        lax.fori_loop(low, high, step, 0)

    barrier = pltpu.get_barrier_semaphore()

    def greet(k):
        peer_seq, peer_grp = peer(k)
        pl.semaphore_signal(
            barrier, inc=1, device_id=(dp, peer_seq, peer_grp), device_id_type=MESH_ID
        )

    def greet_first(k):
        peer_dp, peer_grp = first_peer(k)
        pl.semaphore_signal(
            barrier, inc=1, device_id=(peer_dp, seq, peer_grp), device_id_type=MESH_ID
        )

    loop(1, owner_count, greet)
    loop(2, 2 * dp_count, greet_first)

    all_heads = pl.ds(0, heads)
    given = pl.ds(pl.multiple_of(other * heads, heads), heads)
    kept = pl.ds(pl.multiple_of(grp * heads, heads), heads)
    my_rows = pl.ds(pl.multiple_of(grp * image_rows, image_rows), image_rows)
    other_rows = pl.ds(pl.multiple_of(other * image_rows, image_rows), image_rows)
    local_images = (
        pltpu.make_async_copy(
            image_proj.at[:, 0, kept],
            image_in.at[pl.ds(0, 3), all_heads, my_rows],
            image_recv.at[2],
        ),
        pltpu.make_async_copy(
            image_grad.at[0, kept], image_in.at[3, all_heads, my_rows], image_recv.at[3]
        ),
    )
    for copy in local_images:
        copy.start()
    small = (
        pltpu.make_async_copy(length_any, length, small_recv.at[0]),
        pltpu.make_async_copy(gains_any, gains, small_recv.at[1]),
    )
    for copy in small:
        copy.start()

    def text_ends(step, peer_seq, peer_grp):
        own = pl.ds(step * hps, hps)
        theirs = pl.ds(peer_grp * heads + step * hps, hps)
        return (
            (text_proj.at[:, peer_seq, theirs], text_in.at[pl.ds(0, 3), own, me]),
            (text_grad.at[peer_seq, theirs], text_in.at[3, own, me]),
        )

    def text_stays(step):
        for i, (src, dst) in enumerate(text_ends(step, seq, grp)):
            pltpu.make_async_copy(src, dst, text_recv.at[i, step]).start()

    loop(0, steps, text_stays)
    gain_part[...] = jnp.zeros_like(gain_part)
    pl.semaphore_wait(barrier, owner_count - 1 + 2 * dp_count - 2)

    def remote(src, dst, send, recv, target):
        return pltpu.make_async_remote_copy(
            src_ref=src,
            dst_ref=dst,
            send_sem=send,
            recv_sem=recv,
            device_id=target,
            device_id_type=MESH_ID,
        )

    def text_step(step):
        def send(k):
            peer_seq, peer_grp = peer(k)
            for i, (src, dst) in enumerate(text_ends(step, peer_seq, peer_grp)):
                remote(
                    src,
                    dst,
                    text_send.at[i, step],
                    text_recv.at[i, step],
                    (dp, peer_seq, peer_grp),
                ).start()

        loop(1, owner_count, send)

    loop(0, 1, text_step)

    partner = (dp, seq, other)
    remote(
        image_proj.at[:, 0, given],
        image_in.at[pl.ds(0, 3), all_heads, my_rows],
        image_send.at[0],
        image_recv.at[0],
        partner,
    ).start()
    remote(
        image_grad.at[0, given],
        image_in.at[3, all_heads, my_rows],
        image_send.at[1],
        image_recv.at[1],
        partner,
    ).start()
    loop(1, steps, text_step)

    for copy in local_images + small:
        copy.wait()
    for i, part in enumerate((image_in.at[pl.ds(0, 3), all_heads, other_rows], image_in.at[3, all_heads, other_rows])):
        pltpu.make_async_copy(part, part, image_recv.at[i]).wait()

    total = text_rows + 2 * image_rows
    place = lax.broadcasted_iota(jnp.int32, (1, total), 1)
    bias = jnp.where((place >= text_rows) | (place < length[0]), 0.0, -1.0)

    first_me = dp * 2 + grp
    first_others = gain_first.at[pl.ds(0, 2 * dp_count - 1)]
    second_others = gain_second.at[pl.ds(0, rows_y - 1)]
    third_others = gain_third.at[pl.ds(0, NZ - 1)]
    my_y, my_z = seq // NZ, lax.rem(seq, NZ)

    def gain_hop_one():
        gain_first[first_me] = gain_part[...]

        def send_first(k):
            peer_dp, peer_grp = first_peer(k)
            remote(
                gain_part,
                gain_first.at[first_me],
                gain_send.at[0],
                gain_recv.at[0],
                (peer_dp, seq, peer_grp),
            ).start()

        loop(1, 2 * dp_count, send_first)

    def gain_hop_two():
        pltpu.make_async_copy(first_others, first_others, gain_recv.at[0]).wait()
        mid = jnp.sum(gain_first[...], axis=0)
        gain_mid[...] = mid
        gain_second[my_y] = mid

        def send_second(k):
            remote(
                gain_mid,
                gain_second.at[my_y],
                gain_send.at[1],
                gain_recv.at[1],
                (dp, seq_peer(k * NZ), grp),
            ).start()

        loop(1, rows_y, send_second)

    def gain_hop_three():
        pltpu.make_async_copy(second_others, second_others, gain_recv.at[1]).wait()
        late = jnp.sum(gain_second[...], axis=0)
        gain_late[...] = late
        gain_third[my_z] = late

        def send_third(k):
            remote(
                gain_late,
                gain_third.at[my_z],
                gain_send.at[2],
                gain_recv.at[2],
                (dp, seq_peer(k), grp),
            ).start()

        loop(1, NZ, send_third)

    def give_back(step, low=1, high=owner_count):
        own = pl.ds(step * hps, hps)
        there = pl.ds(grp * heads + step * hps, hps)

        def back_ends(owner):
            return (
                (text_res.at[0, own, owner], text_out.at[seq, there]),
                (text_res.at[pl.ds(1, 3), own, owner], text_proj_grad.at[:, seq, there]),
            )

        def send_back(k):
            peer_seq, peer_grp = peer(k)
            for i, (src, dst) in enumerate(back_ends(peer_seq * 2 + peer_grp)):
                remote(
                    src, dst, back_send.at[i], back_recv.at[i], (dp, peer_seq, peer_grp)
                ).start()

        loop(low, high, send_back)
        if low == 1:
            for i, (src, dst) in enumerate(back_ends(me)):
                pltpu.make_async_copy(src, dst, back_recv.at[i]).start()

    def work(step):
        own = pl.ds(step * hps, hps)
        for i, part in enumerate((text_in.at[pl.ds(0, 3), own], text_in.at[3, own])):
            pltpu.make_async_copy(part, part, text_recv.at[i, step]).wait()
        for j in range(hps):
            head = step * hps + j
            rows = [
                jnp.concatenate(
                    [
                        text_in[c, head].reshape(text_rows, text_in.shape[-1]),
                        image_in[c, head],
                    ],
                    axis=0,
                )
                for c in range(4)
            ]
            results, parts = attend_head(*rows, bias, gains, text_rows)
            gain_part[...] += parts
            for c, result in enumerate(results):
                text_res[c, head] = result[:text_rows].reshape(text_res.shape[2:])
                image_res[c, head] = result[text_rows:]
        pl.when(step < held)(lambda: give_back(step))

    loop(0, steps, work)
    gain_hop_one()

    remote(
        image_res.at[0, all_heads, other_rows],
        image_out.at[0, kept],
        image_back_send.at[0],
        image_back_recv.at[0],
        partner,
    ).start()
    remote(
        image_res.at[pl.ds(1, 3), all_heads, other_rows],
        image_proj_grad.at[:, 0, kept],
        image_back_send.at[1],
        image_back_recv.at[1],
        partner,
    ).start()
    local_results = (
        pltpu.make_async_copy(
            image_res.at[0, all_heads, my_rows], image_out.at[0, kept], image_back_recv.at[2]
        ),
        pltpu.make_async_copy(
            image_res.at[pl.ds(1, 3), all_heads, my_rows],
            image_proj_grad.at[:, 0, kept],
            image_back_recv.at[3],
        ),
    )
    for copy in local_results:
        copy.start()

    loop(held, steps - 1, give_back)
    gain_hop_two()
    third_after = min(THIRD_AFTER, owner_count)
    give_back(steps - 1, 1, third_after)
    gain_hop_three()
    give_back(steps - 1, third_after, owner_count)

    pltpu.make_async_copy(third_others, third_others, gain_recv.at[2]).wait()
    gain = jnp.sum(gain_third[...], axis=0) / samples
    gain_out[0] = gain[:2]
    gain_out[1] = gain[2:]

    for copy in local_results:
        copy.wait()
    sent = (
        (image_in.at[pl.ds(0, 3), all_heads, my_rows], image_send.at[0]),
        (image_in.at[3, all_heads, my_rows], image_send.at[1]),
        (image_out.at[0, kept], image_back_send.at[0]),
        (image_proj_grad.at[:, 0, kept], image_back_send.at[1]),
        (image_out.at[0, given], image_back_recv.at[0]),
        (image_proj_grad.at[:, 0, given], image_back_recv.at[1]),
        (first_others, gain_send.at[0]),
        (second_others, gain_send.at[1]),
        (third_others, gain_send.at[2]),
        (text_out, back_recv.at[0]),
        (text_proj_grad, back_recv.at[1]),
        (text_res.at[0, :, pl.ds(0, owner_count - 1)], back_send.at[0]),
        (text_res.at[pl.ds(1, 3), :, pl.ds(0, owner_count - 1)], back_send.at[1]),
    )
    for part, semaphore in sent:
        pltpu.make_async_copy(part, part, semaphore).wait()

    def sent_text(step):
        own = pl.ds(step * hps, hps)
        others = pl.ds(0, owner_count - 1)
        for i, part in enumerate((text_in.at[pl.ds(0, 3), own, others], text_in.at[3, own, others])):
            pltpu.make_async_copy(part, part, text_send.at[i, step]).wait()

    loop(0, steps, sent_text)


def put_out(count, *refs):
    results, outs, held = refs[:count], refs[count : 2 * count], refs[2 * count : 3 * count]
    semaphores = refs[-1]
    reads, writes = [], []
    for i in range(count):
        long = max(range(results[i].ndim - 2), key=lambda d: results[i].shape[d])
        pieces = PIECES if results[i].shape[long] % PIECES == 0 else 1
        size = results[i].shape[long] // pieces
        for j in range(pieces):
            part = (slice(None),) * long + (pl.ds(j * size, size),)
            src, mid, dst = results[i].at[part], held[i].at[part], outs[i].at[part]
            reads.append(pltpu.make_async_copy(src, mid, semaphores.at[0, i, j]))
            writes.append(pltpu.make_async_copy(mid, dst, semaphores.at[1, i, j]))
    for copy in reads:
        copy.start()
    for read, write in zip(reads, writes):
        read.wait()
        write.start()
    for copy in writes:
        copy.wait()


def per_device(sizes, text_proj, image_proj, text_grad, image_grad, text_lengths, norm_gains):
    dp_count, seq_count, _ = sizes
    _, _, head_count, text_group, size = text_proj.shape
    image_rows = image_proj.shape[3]
    heads = head_count // 2
    owners = seq_count * 2
    steps = heads // HEADS_PER_STEP
    bf16 = jnp.bfloat16
    anywhere = pl.BlockSpec(memory_space=pl.ANY)
    text_shape = (4, heads, owners, text_group, size)
    image_shape = (4, heads, 2 * image_rows, size)
    dma = pltpu.SemaphoreType.DMA
    total = owners * text_group + 2 * image_rows
    results = pl.pallas_call(
        functools.partial(kernel, sizes),
        out_shape=(
            jax.ShapeDtypeStruct(text_grad.shape, bf16),
            jax.ShapeDtypeStruct(text_proj.shape, bf16),
            jax.ShapeDtypeStruct(image_grad.shape, bf16),
            jax.ShapeDtypeStruct(image_proj.shape, bf16),
            jax.ShapeDtypeStruct(norm_gains.shape, jnp.float32),
        ),
        in_specs=[anywhere] * 6,
        out_specs=(anywhere,) * 4 + (pl.BlockSpec(memory_space=pltpu.VMEM),),
        scratch_shapes=[
            pltpu.VMEM(text_shape, bf16),
            pltpu.VMEM(image_shape, bf16),
            pltpu.VMEM(text_shape, bf16),
            pltpu.VMEM(image_shape, bf16),
            pltpu.VMEM((4, size), jnp.float32),
            pltpu.VMEM((2 * dp_count, 4, size), jnp.float32),
            pltpu.VMEM((4, size), jnp.float32),
            pltpu.VMEM((seq_count // NZ, 4, size), jnp.float32),
            pltpu.VMEM((4, size), jnp.float32),
            pltpu.VMEM((NZ, 4, size), jnp.float32),
            pltpu.SMEM((1,), jnp.int32),
            pltpu.VMEM(norm_gains.shape, jnp.float32),
            dma((2, steps)),
            dma((2, steps)),
            dma((2,)),
            dma((4,)),
            dma((2,)),
            dma((2,)),
            dma((2,)),
            dma((4,)),
            dma((3,)),
            dma((3,)),
            dma((2,)),
        ],
        compiler_params=pltpu.CompilerParams(
            collective_id=0, has_side_effects=True, vmem_limit_bytes=VMEM_LIMIT
        ),
        cost_estimate=pl.CostEstimate(
            flops=heads * 12 * total * total * size,
            bytes_accessed=2 * 8 * heads * total * size * 2,
            transcendentals=heads * total * total,
        ),
    )(text_proj, text_grad, image_proj, image_grad, text_lengths, norm_gains)
    text_out, text_proj_grad, image_out, image_proj_grad, gain_grad = pl.pallas_call(
        functools.partial(put_out, len(results)),
        out_shape=tuple(jax.ShapeDtypeStruct(r.shape, r.dtype) for r in results),
        in_specs=[anywhere] * len(results),
        out_specs=(anywhere,) * len(results),
        scratch_shapes=[pltpu.VMEM(r.shape, r.dtype) for r in results] + [dma((2, len(results), PIECES))],
        compiler_params=pltpu.CompilerParams(vmem_limit_bytes=VMEM_LIMIT),
    )(*results)
    return text_out, image_out, text_proj_grad, image_proj_grad, gain_grad


def solution(mesh):
    dp_count, seq_count = mesh.shape["dp"], mesh.shape["seq"]
    text_proj = P(None, "dp", None, ("seq", "grp"), None)
    image_proj = P(None, ("dp", "seq"), None, "grp", None)
    text_grad = P("dp", None, ("seq", "grp"), None)
    image_grad = P(("dp", "seq"), None, "grp", None)

    def run(*args):
        sizes = (dp_count, seq_count, args[4].shape[0])
        return jax.shard_map(
            functools.partial(per_device, sizes),
            mesh=mesh,
            in_specs=(text_proj, image_proj, text_grad, image_grad, P(("dp", "seq")), P()),
            out_specs=(text_grad, image_grad, text_proj, image_proj, P()),
            check_vma=False,
        )(*args)

    return run
```
